32 devices in a mesh: tm: 8 (over z, core), blk: 4 (over y, x).
Axes of the slice: x: 2, y: 2, z: 4, core: 2. Of those that a mesh axis runs over, the one named last changes fastest.
Arguments:
- queries: bfloat16 [32, 9, 3840], P('blk'), may hold values from -6 to 6
- index_regions: bfloat16 [4, 9, 512, 3840], P('blk', None, 'tm'), may hold values from -0.09375 to 0.09375
- conv_one: float32 [16, 9], replicated, may hold values from -2 to 2
- bias_one: float32 [16], replicated, may hold values from -3 to 3
- conv_two: float32 [16, 9], replicated, may hold values from -0.5 to 0.5
- bias_two: float32 [1], replicated, may hold values from -3 to 3
- index_lengths: int32 [4, 8], P('blk'), may hold values from 1 to 128, 512 in all within a row
- query_lengths: int32 [4], replicated, may hold values from 1 to 16, 32 in all
Outputs:
- scores: float32 [4, 4, 8], P('blk')
The draws below stay inside these ranges and needn't reach their ends.
Inputs may be any that keep to these rules, and one draw needn't show every extreme that they name: Each row of index_lengths lists the frame counts of the index videos of one partition in time order; they sum to 512, and some video has exactly 128 frames. query_lengths lists the frame counts of the query clips in time order; they sum to 32, and some clip has exactly 16 frames.
All inputs are finite; a program needn't handle non-finite values.
Results may differ from the reference program's by a relative error of at most 0.0003.
Values may be sent and summed in bfloat16 or wider, within the bound.
No kernel may reach another device: no remote copies, remote signals or barrier semaphores. Data moves between devices by JAX's collectives and lax.ppermute only.
A program may use at most 64 MiB of HBM per device.

```python
import math
import jax
import jax.numpy as jnp
import numpy as np
from jax import lax

D = 3840
R = 9
CH = 16
F_DEV = 64
VIDLEN = 64
CLIPLEN = 8
NB = 4
NQ = 32
NI = 512
NVI = 8
NVQ = 4
N_TM = 8


def block_levels(rng, dims, split, least, top_value):
    factor_of = 1.0
    for dim, blocks in split:
        heights = jax.random.uniform(jax.random.fold_in(jax.random.fold_in(rng, 6), dim), (blocks,), jnp.float32, least / len(split), top_value / len(split))
        factor_of = factor_of * jnp.repeat(jnp.exp(heights), dims[dim] // blocks).reshape((-1,) + (1,) * (len(dims) - 1 - dim))
    return factor_of


def profile(amount, total, limit, skew):
    portions = [(1 << 20) // math.isqrt(rank ** skew) + 1 for rank in range(2, amount + 1)]
    rest, given = total - limit - (amount - 1), [1] * (amount - 1)
    while rest > 0:
        free = [i for i in range(amount - 1) if given[i] < limit]
        whole, left = sum([portions[i] for i in free]), rest
        for i in free:
            extra = min(limit - given[i], max(1, left * portions[i] // whole), rest)
            given[i] = given[i] + extra
            rest = rest - extra
    return np.array([limit] + given)


def ragged(key, number_of, total, reach, slope):
    if number_of == 2:
        one = jax.random.randint(key, (), max(1, total - reach), min(reach, total - 1) + 1)
        return jnp.stack([one, total - one])
    sizes = jnp.asarray(profile(number_of, total, reach, slope), jnp.int32)
    twos = (number_of - 1) // 2
    donor, sink = sizes[1:1 + 2 * twos:2], sizes[2:2 + 2 * twos:2]
    margin = jnp.minimum(donor - 1, reach - sink)
    passed = jax.random.randint(jax.random.fold_in(key, 1), (twos,), 0, 1 << 20) % (margin + 1)
    sizes = sizes.at[1:1 + 2 * twos:2].set(donor - passed).at[2:2 + 2 * twos:2].set(sink + passed)
    return sizes[jax.random.permutation(jax.random.fold_in(key, 2), number_of)]


def noise(rng, shape, spread, reach, pieces=(), kind=jnp.bfloat16):
    result = jax.random.normal(rng, shape, jnp.float32) * spread
    if len(pieces) > 0:
        result = block_levels(rng, shape, pieces, -0.22, 0.18) * result
    return jnp.clip(result, min=-reach, max=reach).astype(kind)


def setup_inputs(seed: int = 0) -> dict:
    seeds = jax.random.split(jax.random.key(seed), 9)
    queries = noise(seeds[0], (NQ, R, D), 1.0, 6.0, ((0, 4),))
    index_regions = noise(seeds[1], (NB, R, NI, D), D ** -0.5, 0.09375, ((0, 4), (2, 8)))
    conv_one = noise(seeds[2], (CH, 9), 9 ** -0.5, 2.0, (), jnp.float32)
    bias_one = noise(seeds[3], (CH,), 0.5, 3.0, (), jnp.float32)
    conv_two = noise(seeds[4], (CH, 9), (9 * CH) ** -0.5, 0.5, (), jnp.float32)
    bias_two = noise(seeds[5], (1,), 1.0, 3.0, (), jnp.float32)
    index_lengths = jax.vmap(lambda own: ragged(own, NVI, NI, 2 * VIDLEN, 1))(jax.random.split(seeds[6], NB)).reshape((NB, NVI)).astype(jnp.int32)
    query_lengths = ragged(seeds[7], NVQ, NQ, 2 * CLIPLEN, 1).astype(jnp.int32)
    return {"queries": queries, "index_regions": index_regions, "conv_one": conv_one, "bias_one": bias_one, "conv_two": conv_two, "bias_two": bias_two, "index_lengths": index_lengths, "query_lengths": query_lengths}


very_low = -1.0e9
highest = lax.Precision.HIGHEST


def segment_ids(lengths, positions, extent):
    starts = jnp.cumsum(lengths) - lengths
    inside = (positions >= 0) & (positions < extent)
    counts = jnp.sum((positions[:, None] >= starts[None, :]).astype(jnp.int32), axis=1) - 1
    return jnp.where(inside, counts, -1).astype(jnp.int32)


def frame_similarity(block, index_rows):
    row_count, regions, feature_width = block.shape
    col_count = index_rows.shape[1]
    products = lax.dot_general(block.reshape(row_count * regions, feature_width), index_rows.reshape(regions * col_count, feature_width), (((1,), (1,)), ((), ())), precision=highest, preferred_element_type=jnp.float32)
    products = products.reshape(row_count, regions, regions, col_count)
    return jnp.mean(jnp.max(products, axis=2), axis=1)


def neighbour_masks(ids, extent):
    centre = ids[1:extent + 1]
    return [((ids[shift_by:shift_by + extent] == centre) & (centre >= 0)).astype(jnp.float32) for shift_by in range(3)]


def stencil_taps(source, row_ids, col_ids):
    height = source.shape[-2] - 2
    breadth = source.shape[-1] - 2
    row_masks = neighbour_masks(row_ids, height)
    col_masks = neighbour_masks(col_ids, breadth)
    shifted = []
    for row_step in range(3):
        for col_step in range(3):
            window = source[..., row_step:row_step + height, col_step:col_step + breadth]
            shifted.append(window * (row_masks[row_step][:, None] * col_masks[col_step][None, :]))
    return jnp.stack(shifted)


def refine(similar, row_ids, col_ids, conv_one, bias_one, conv_two, bias_two):
    shifted = stencil_taps(similar, row_ids, col_ids)
    hidden = jnp.einsum("ct,tij->cij", conv_one, shifted, precision=highest) + bias_one[:, None, None]
    hidden = jax.nn.relu(hidden)
    shifted = stencil_taps(hidden, row_ids[1:-1], col_ids[1:-1])
    return jnp.einsum("ct,tcij->ij", conv_two, shifted, precision=highest) + bias_two[0]


def reference(queries, index_regions, conv_one, bias_one, conv_two, bias_two, index_lengths, query_lengths):
    query_wide = jnp.pad(queries.astype(jnp.float32), ((2, 2), (0, 0), (0, 0)))
    row_ids = segment_ids(query_lengths, jnp.arange(NQ + 4, dtype=jnp.int32) - 2, NQ)
    clip_ids = segment_ids(query_lengths, jnp.arange(NQ, dtype=jnp.int32), NQ)
    members = (jnp.arange(NVQ, dtype=jnp.int32)[:, None] == clip_ids[None, :]).astype(jnp.float32)

    def one_partition(pair):
        regions_all, lengths = pair
        index_wide = jnp.pad(regions_all.astype(jnp.float32), ((0, 0), (2, 2), (0, 0)))
        col_all = segment_ids(lengths, jnp.arange(NI + 4, dtype=jnp.int32) - 2, NI)

        def one_block(block_num):
            first_col = (block_num * F_DEV).astype(jnp.int32)
            index_rows = lax.dynamic_slice_in_dim(index_wide, first_col, F_DEV + 4, 1)
            col_ids = lax.dynamic_slice_in_dim(col_all, first_col, F_DEV + 4, 0)
            refined = refine(frame_similarity(query_wide, index_rows), row_ids, col_ids, conv_one, bias_one, conv_two, bias_two)
            holders = col_ids[2:-2][:, None] == jnp.arange(NVI, dtype=jnp.int32)[None, :]
            return jnp.max(jnp.where(holders[None, :, :], refined[:, :, None], very_low), axis=1)

        tables = lax.map(one_block, jnp.arange(N_TM, dtype=jnp.int32))
        global_max = jnp.max(tables, axis=0)
        totals = jnp.dot(members, global_max, precision=highest, preferred_element_type=jnp.float32)
        return totals / query_lengths.astype(jnp.float32)[:, None]

    return lax.map(one_partition, (index_regions, index_lengths))
```

```python
import functools
import jax
import jax.numpy as jnp
from jax import lax
from jax.experimental import pallas as pl
from jax.experimental.pallas import tpu as pltpu
from jax.sharding import PartitionSpec as P

very_low = -1000000000.0
highest = lax.Precision.HIGHEST
LANES = 128
SUBLANES = 8
VMEM_LIMIT = 32 * 1024 * 1024


def inner(a, b, precision=None):
    return lax.dot_general(
        a, b, (((1,), (1,)), ((), ())), precision=precision, preferred_element_type=jnp.float32
    )


def stacked(refs):
    return refs[0][...] if len(refs) == 1 else jnp.concatenate([r[...] for r in refs], axis=0)


def region_maxima(index_ref, outside_ref, inside_ref, parts, parity):
    regions, frames, _ = index_ref.shape
    own = None
    border = None
    for first, size, refs in parts:
        block = stacked(refs)
        at = pl.ds(first, size)
        rows = index_ref[:, :, at].reshape(regions * frames, size)
        ends = jnp.concatenate([outside_ref[:, at], inside_ref[:, at]], axis=0)
        products = inner(rows, block)
        sides = inner(ends, block)
        own = products if own is None else own + products
        border = sides if border is None else border + sides
    width = own.shape[1]
    maxima = jnp.max(own.reshape(regions, frames, width), axis=0)
    row = lax.broadcasted_iota(jnp.int32, border.shape, 0)
    count = 2 * regions

    def end_max(side, j):
        picked = (row >= side * count) & (row < (side + 1) * count) & (row % 2 == j)
        return jnp.max(jnp.where(picked, border, -jnp.inf), axis=0, keepdims=True)

    ends = [[end_max(side, j) for j in range(2)] for side in range(2)]
    even = parity == 0
    after = [jnp.where(even, ends[1][j], ends[0][j]) for j in range(2)]
    before = [jnp.where(even, ends[0][j], ends[1][j]) for j in range(2)]
    slot = lax.broadcasted_iota(jnp.int32, (SUBLANES, width), 0)
    last = jnp.zeros((SUBLANES, width), jnp.float32)
    for place, value in ((0, after[0]), (1, after[1]), (6, before[0]), (7, before[1])):
        last = jnp.where(slot == place, value, last)
    return maxima, last


def region_mean(maxima, last, blocks, block_rows, regions, total_rows):
    frames, width = maxima.shape
    gap = jnp.zeros((LANES - frames - 2 * SUBLANES, width), jnp.float32)
    table = jnp.concatenate([maxima, last, gap, last], axis=0)
    row = lax.broadcasted_iota(jnp.int32, (total_rows, width), 0)
    lane = lax.broadcasted_iota(jnp.int32, (total_rows, width), 1)
    per_block = regions * block_rows
    picked = jnp.zeros((total_rows, width), jnp.bool_)
    for number, block in enumerate(blocks):
        inside = (lane >= number * per_block) & (lane < (number + 1) * per_block)
        picked = picked | (inside & (row == block * block_rows + lane % block_rows))
    return inner(picked.astype(jnp.float32), table, highest)


def ids_at(lengths, count, positions):
    found = jnp.full(positions.shape, -1, jnp.int32)
    start = jnp.int32(0)
    for k in range(count):
        found = found + (positions >= start).astype(jnp.int32)
        start = start + lengths(k)
    return found


def refine_and_best(
    similar, first_frame, extent, frames, video_ref, clip_ref, one_ref, bias_one_ref, two_ref, bias_two_ref
):
    total_rows = similar.shape[0]
    channels = bias_one_ref.shape[0]
    videos = video_ref.shape[1]
    shape = (total_rows, LANES)
    lane = lax.broadcasted_iota(jnp.int32, shape, 1)
    row = lax.broadcasted_iota(jnp.int32, shape, 0)
    offset = jnp.where(lane < frames + SUBLANES, lane, lane - LANES)
    position = first_frame + offset
    known = (offset >= -2) & (offset < frames + 2) & (position >= 0) & (position < extent)
    col_ids = jnp.where(known, ids_at(lambda k: video_ref[0, k], videos, position), -1)
    row_ids = ids_at(lambda k: clip_ref[k], clip_ref.shape[0], row)

    def rolled(x, step, axis):
        return x if step == 0 else pltpu.roll(x, (-step) % x.shape[axis], axis)

    steps = (-1, 0, 1)
    col_mask = [
        ((rolled(col_ids, b, 1) == col_ids) & (col_ids >= 0)).astype(jnp.float32) for b in steps
    ]
    row_mask = [
        (
            (rolled(row_ids, a, 0) == row_ids) & (row + a >= 0) & (row + a < total_rows)
        ).astype(jnp.float32)
        for a in steps
    ]
    across = [rolled(similar, b, 1) * col_mask[b + 1] for b in steps]
    taps = []
    for a in steps:
        for b in steps:
            tap = across[b + 1]
            taps.append(tap if a == 0 else rolled(tap, a, 0) * row_mask[a + 1])
    piece = 2 * SUBLANES
    gathered = [[] for _ in range(9)]
    for top in range(0, total_rows, piece):
        source = [tap[top : top + piece] for tap in taps]
        sums = [None] * 9
        for c in range(channels):
            hidden = one_ref[c, 0] * source[0] + bias_one_ref[c]
            for t in range(1, 9):
                hidden = hidden + one_ref[c, t] * source[t]
            hidden = jnp.maximum(hidden, 0.0)
            for t in range(9):
                term = two_ref[c, t] * hidden
                sums[t] = term if c == 0 else sums[t] + term
        for t in range(9):
            gathered[t].append(sums[t])
    gathered = [jnp.concatenate(parts, axis=0) for parts in gathered]
    refined = jnp.full(shape, bias_two_ref[0], jnp.float32)
    for b in steps:
        column = gathered[3 + b + 1]
        for a in (-1, 1):
            column = column + rolled(gathered[3 * (a + 1) + b + 1], a, 0) * row_mask[a + 1]
        refined = refined + rolled(column, b, 1) * col_mask[b + 1]
    own_ids = jnp.where((offset >= 0) & (offset < frames), col_ids, -1)
    best = jnp.full(shape, very_low, jnp.float32)
    for v in range(videos):
        top_value = jnp.max(
            jnp.where(own_ids == v, refined, very_low), axis=1, keepdims=True
        )
        best = jnp.where(lane == v, top_value, best)
    return best[:, :videos]


def parts_of(layout, refs, parity, depth):
    half = depth // 2
    parts = []
    taken = 0
    for which, count in layout:
        pieces = refs[taken : taken + count]
        taken += count
        if which is None:
            parts.append((0, depth, pieces))
        else:
            side = parity if which == 0 else 1 - parity
            parts.append((pl.multiple_of(side * half, LANES), half, pieces))
    return parts


def early_kernel(layout, index_ref, outside_ref, inside_ref, *refs):
    *pieces, maxima_ref, last_ref = refs
    parity = lax.axis_index("tm") % 2
    parts = parts_of(layout, pieces, parity, index_ref.shape[2])
    maxima, last = region_maxima(index_ref, outside_ref, inside_ref, parts, parity)
    maxima_ref[...] = maxima
    last_ref[...] = last


def late_kernel(
    layout, blocks_of, early_of, block_rows, total_rows, extent,
    video_ref, clip_ref, one_ref, bias_one_ref, two_ref, bias_two_ref,
    index_ref, outside_ref, inside_ref, *refs,
):
    *refs, best_ref = refs
    regions, frames, depth = index_ref.shape
    time_index = lax.axis_index("tm")
    parity = time_index % 2
    position = lax.axis_index("blk")
    early = 0 if early_of is None else 2
    parts = parts_of(layout, refs[early:], parity, depth)
    maxima, last = region_maxima(index_ref, outside_ref, inside_ref, parts, parity)
    mean_of = functools.partial(
        region_mean, block_rows=block_rows, regions=regions, total_rows=total_rows
    )
    similar = mean_of(maxima, last, blocks_of(parity, position))
    if early:
        similar = similar + mean_of(refs[0][...], refs[1][...], early_of(parity, position))
    similar = similar * (1.0 / regions)
    best_ref[...] = refine_and_best(
        similar, time_index * frames, extent, frames,
        video_ref, clip_ref, one_ref, bias_one_ref, two_ref, bias_two_ref,
    )


def score_kernel(clip_ref, *refs):
    *tables, scores_ref = refs
    best = tables[0][...]
    for table in tables[1:]:
        best = jnp.maximum(best, table[...])
    rows = best.shape[0]
    clips = clip_ref.shape[0]
    row_ids = ids_at(lambda k: clip_ref[k], clips, lax.broadcasted_iota(jnp.int32, best.shape, 0))
    for c in range(clips):
        total = jnp.sum(jnp.where(row_ids == c, best, 0.0), axis=0, keepdims=True)
        scores_ref[0, c : c + 1, :] = total / clip_ref[c].astype(jnp.float32)


def in_vmem():
    return pl.BlockSpec(memory_space=pltpu.VMEM)


def in_smem():
    return pl.BlockSpec(memory_space=pltpu.SMEM)


def shards(
    queries, index_regions, conv_one, bias_one, conv_two, bias_two, index_lengths, query_lengths
):
    cycle_size = lax.axis_size("blk")
    time_size = lax.axis_size("tm")
    block_rows, regions, depth = queries.shape
    total_rows = block_rows * cycle_size
    index = index_regions[0]
    frames = index.shape[1]
    extent = frames * time_size
    videos = index_lengths.shape[1]
    odd = lax.axis_index("tm") % 2 == 1
    half = depth // 2
    width = regions * block_rows

    def sent(x, source):
        pairs = []
        for t in range(time_size):
            for b in range(cycle_size):
                found = source(t, b)
                if found is not None and 0 <= found[0] < time_size:
                    pairs.append((found[0] * cycle_size + found[1], t * cycle_size + b))
        return lax.ppermute(x, ("tm", "blk"), pairs)

    def beside(t, b):
        return t ^ 1, b

    def crossing(t, b):
        return (t - 1, b) if t % 2 == 0 else (t + 1, b)

    def ends():
        head = index[:, :2].reshape(2 * regions, depth)
        tail = index[:, frames - 2 :].reshape(2 * regions, depth)
        outer = jnp.where(odd, tail, head)
        inner_side = jnp.where(odd, head, tail)
        return sent(outer, crossing), sent(inner_side, beside)

    flat = jnp.swapaxes(queries, 0, 1).reshape(width, depth)
    scalars = (index_lengths, query_lengths, conv_one, bias_one, conv_two, bias_two)
    params = pltpu.CompilerParams(vmem_limit_bytes=VMEM_LIMIT)
    if cycle_size == 4:
        first = jnp.where(odd, flat[:, :half], flat[:, half:])
        second = jnp.where(odd, flat[:, half:], flat[:, :half])

        def near(t, b):
            return (t, b ^ 1) if t % 2 == 0 else (t, b ^ 2)

        def far(t, b):
            return (t ^ 1, b ^ 1) if t % 2 == 0 else (t ^ 1, b ^ 2)

        near_first = sent(first, near)
        near_second = sent(second, near)
        outside, inside = ends()
        far_first = sent(near_first, far)
        next_first = sent(near_first, beside)
        next_second = sent(near_second, beside)
        early = pl.pallas_call(
            functools.partial(early_kernel, ((1, 2), (0, 2))),
            in_specs=[in_vmem()] * 7,
            out_specs=[in_vmem()] * 2,
            out_shape=[
                jax.ShapeDtypeStruct((frames, 2 * width), jnp.float32),
                jax.ShapeDtypeStruct((SUBLANES, 2 * width), jnp.float32),
            ],
            compiler_params=params,
            name="early_products",
        )(index, outside, inside, first, near_first, second, near_second)
        far_second = sent(far_first, beside)

        def own_and_near(parity, b):
            return b, b ^ (1 + parity)

        def next_and_far(parity, b):
            return b ^ (2 - parity), b ^ 3

        layout, pieces = ((0, 2), (1, 2)), (next_first, far_first, next_second, far_second)
        blocks_of, early_of = next_and_far, own_and_near
    else:
        outside, inside = ends()
        every = lax.all_gather(flat, "blk")
        early = ()
        layout, pieces = ((None, cycle_size),), [every[b] for b in range(cycle_size)]
        blocks_of, early_of = (lambda parity, b: tuple(range(cycle_size))), None
    best = pl.pallas_call(
        functools.partial(
            late_kernel, layout, blocks_of, early_of, block_rows, total_rows, extent
        ),
        in_specs=[in_smem()] * 6 + [in_vmem()] * (3 + len(early) + len(pieces)),
        out_specs=in_vmem(),
        out_shape=jax.ShapeDtypeStruct((total_rows, videos), jnp.float32),
        compiler_params=params,
        name="late_products",
    )(*scalars, index, outside, inside, *early, *pieces)
    step = 1
    while step < time_size:
        other = sent(best, lambda t, b: (t ^ step, b))
        if 2 * step < time_size:
            best = jnp.maximum(best, other)
        step *= 2
    return pl.pallas_call(
        score_kernel,
        in_specs=[in_smem()] + [in_vmem()] * 2,
        out_specs=in_vmem(),
        out_shape=jax.ShapeDtypeStruct((1, query_lengths.shape[0], videos), jnp.float32),
        compiler_params=params,
        name="clip_scores",
    )(query_lengths, best, other)


def solution(mesh):
    placed = (
        P("blk", None, None),
        P("blk", None, "tm", None),
        P(),
        P(),
        P(),
        P(),
        P("blk", None),
        P(),
    )
    return jax.shard_map(
        shards, mesh=mesh, in_specs=placed, out_specs=P("blk", None, None), check_vma=False
    )
```

```python
import functools
import jax
import jax.numpy as jnp
from jax import lax
from jax.experimental import pallas as pl
from jax.experimental.pallas import tpu as pltpu
from jax.sharding import PartitionSpec as P

very_low = -1000000000.0
highest = lax.Precision.HIGHEST
LANES = 128
SUBLANES = 8
EDGE = 8
VMEM_LIMIT = 32 * 1024 * 1024


def inner(a, b, precision=None):
    return lax.dot_general(
        a, b, (((1,), (1,)), ((), ())), precision=precision, preferred_element_type=jnp.float32
    )


def stacked(refs):
    return refs[0][...] if len(refs) == 1 else jnp.concatenate([r[...] for r in refs], axis=0)


def products_of(index_ref, parts):
    regions, frames, _ = index_ref.shape
    total = None
    for first, size, refs in parts:
        rows = index_ref[:, :, pl.ds(first, size)].reshape(regions * frames, size)
        products = inner(rows, stacked(refs))
        total = products if total is None else total + products
    return total


def region_maxima(products, regions):
    return jnp.max(products.reshape(regions, -1, products.shape[1]), axis=0)


def region_mean(maxima, blocks, block_rows, regions, total_rows):
    frames, width = maxima.shape
    table = jnp.concatenate([maxima, jnp.zeros((LANES - frames, width), jnp.float32)], axis=0)
    row = lax.broadcasted_iota(jnp.int32, (total_rows, width), 0)
    lane = lax.broadcasted_iota(jnp.int32, (total_rows, width), 1)
    per_block = regions * block_rows
    picked = jnp.zeros((total_rows, width), jnp.bool_)
    for number, block in enumerate(blocks):
        inside = (lane >= number * per_block) & (lane < (number + 1) * per_block)
        picked = picked | (inside & (row == block * block_rows + lane % block_rows))
    return inner(picked.astype(jnp.float32), table, highest)


def ids_at(lengths, count, positions):
    found = jnp.full(positions.shape, -1, jnp.int32)
    start = jnp.int32(0)
    for k in range(count):
        found = found + (positions >= start).astype(jnp.int32)
        start = start + lengths(k)
    return found


def rolled(x, step, axis):
    return x if step == 0 else pltpu.roll(x, (-step) % x.shape[axis], axis)


def video_ids(video_ref, position, known):
    return jnp.where(known, ids_at(lambda k: video_ref[0, k], video_ref.shape[1], position), -1)


def refine(similar, position, col_ids, clip_ref, one_ref, bias_one_ref, two_ref, bias_two_ref):
    total_rows, _ = shape = similar.shape
    channels = bias_one_ref.shape[0]
    row = lax.broadcasted_iota(jnp.int32, shape, 0)
    row_ids = ids_at(lambda k: clip_ref[k], clip_ref.shape[0], row)
    steps = (-1, 0, 1)
    col_mask = [
        (
            (rolled(col_ids, b, 1) == col_ids)
            & (col_ids >= 0)
            & (rolled(position, b, 1) == position + b)
        ).astype(jnp.float32)
        for b in steps
    ]
    row_mask = [
        (
            (rolled(row_ids, a, 0) == row_ids) & (row + a >= 0) & (row + a < total_rows)
        ).astype(jnp.float32)
        for a in steps
    ]
    across = [rolled(similar, b, 1) * col_mask[b + 1] for b in steps]
    taps = []
    for a in steps:
        for b in steps:
            tap = across[b + 1]
            taps.append(tap if a == 0 else rolled(tap, a, 0) * row_mask[a + 1])
    piece = 2 * SUBLANES
    gathered = [[] for _ in range(9)]
    for top in range(0, total_rows, piece):
        source = [tap[top : top + piece] for tap in taps]
        sums = [None] * 9
        for c in range(channels):
            hidden = one_ref[c, 0] * source[0] + bias_one_ref[c]
            for t in range(1, 9):
                hidden = hidden + one_ref[c, t] * source[t]
            hidden = jnp.maximum(hidden, 0.0)
            for t in range(9):
                term = two_ref[c, t] * hidden
                sums[t] = term if c == 0 else sums[t] + term
        for t in range(9):
            gathered[t].append(sums[t])
    gathered = [jnp.concatenate(parts, axis=0) for parts in gathered]
    refined = jnp.full(shape, bias_two_ref[0], jnp.float32)
    for b in steps:
        column = gathered[3 + b + 1]
        for a in (-1, 1):
            column = column + rolled(gathered[3 * (a + 1) + b + 1], a, 0) * row_mask[a + 1]
        refined = refined + rolled(column, b, 1) * col_mask[b + 1]
    return refined


def video_best(refined, ids, videos, first_lane):
    lane = lax.broadcasted_iota(jnp.int32, (refined.shape[0], LANES), 1)
    best = jnp.full(lane.shape, very_low, jnp.float32)
    for v in range(videos):
        top = jnp.max(jnp.where(ids == v, refined, very_low), axis=1, keepdims=True)
        best = jnp.where(lane == first_lane + v, top, best)
    return best


def message_lanes(time_size, videos):
    table = time_size * EDGE
    lanes = -(-(table + videos) // LANES) * LANES
    assert table // LANES == lanes // LANES - 1
    return table, lanes


def halves(depth, layout):
    half = depth // 2
    parity = lax.axis_index("tm") % 2
    sides = (parity, 1 - parity)
    return [(pl.multiple_of(sides[k] * half, LANES), half, refs) for k, refs in layout]


def own_kernel(index_ref, first_ref, second_ref, maxima_ref):
    parts = halves(index_ref.shape[2], ((1, [first_ref]), (0, [second_ref])))
    maxima_ref[...] = region_maxima(products_of(index_ref, parts), index_ref.shape[0])


def near_kernel(
    block_rows, total_rows, index_ref, first_ref, second_ref, own_ref, similar_ref
):
    regions = index_ref.shape[0]
    parts = halves(index_ref.shape[2], ((1, [first_ref]), (0, [second_ref])))
    near = region_maxima(products_of(index_ref, parts), regions)
    block = lax.axis_index("blk")
    parity = lax.axis_index("tm") % 2
    mean_of = functools.partial(
        region_mean, block_rows=block_rows, regions=regions, total_rows=total_rows
    )
    similar_ref[...] = mean_of(own_ref[...], (block,)) + mean_of(near, (block ^ (1 + parity),))


def half_kernel(index_ref, next_ref, far_ref, products_ref):
    parts = halves(index_ref.shape[2], ((0, [next_ref, far_ref]),))
    products_ref[...] = products_of(index_ref, parts)


def late_kernel(
    count, block_rows, total_rows,
    video_ref, clip_ref, one_ref, bias_one_ref, two_ref, bias_two_ref, index_ref, *refs,
):
    *refs, message_ref = refs
    regions, frames, depth = index_ref.shape
    videos = video_ref.shape[1]
    time_index = lax.axis_index("tm")
    mean_of = functools.partial(
        region_mean, block_rows=block_rows, regions=regions, total_rows=total_rows
    )
    if count:
        products = products_of(index_ref, ((0, depth, refs),))
        similar = mean_of(region_maxima(products, regions), tuple(range(count)))
    else:
        next_ref, far_ref, products_ref, similar_ref = refs
        parts = halves(depth, ((1, [next_ref, far_ref]),))
        products = products_ref[...] + products_of(index_ref, parts)
        parity = time_index % 2
        block = lax.axis_index("blk")
        blocks = (block ^ (2 - parity), block ^ 3)
        similar = similar_ref[...] + mean_of(region_maxima(products, regions), blocks)
    similar = similar * (1.0 / regions)
    lane = lax.broadcasted_iota(jnp.int32, similar.shape, 1)
    place = time_index * frames + lane
    col_ids = video_ids(video_ref, place, lane < frames)
    refined = refine(
        similar, place, col_ids, clip_ref, one_ref, bias_one_ref, two_ref, bias_two_ref
    )
    inner_ids = jnp.where((lane >= 2) & (lane < frames - 2), col_ids, -1)
    table, lanes = message_lanes(lax.axis_size("tm"), videos)
    best = video_best(refined, inner_ids, videos, table % LANES)
    edges = jnp.where(lane < EDGE // 2, similar, rolled(similar, frames - EDGE, 1))
    edges = jnp.where(lane < EDGE, edges, very_low)
    slot = time_index * EDGE
    edges = pltpu.roll(edges, slot % LANES, 1)
    for k in range(lanes // LANES):
        tile = jnp.where(slot // LANES == k, edges, very_low)
        if k == table // LANES:
            tile = jnp.maximum(tile, best)
        message_ref[:, k * LANES : (k + 1) * LANES] = tile


def score_kernel(
    frames, time_size, video_ref, clip_ref, one_ref, bias_one_ref, two_ref, bias_two_ref, *refs
):
    *messages, scores_ref = refs
    message = messages[0][...]
    for other in messages[1:]:
        message = jnp.maximum(message, other[...])
    videos = video_ref.shape[1]
    clips = clip_ref.shape[0]
    table, lanes = message_lanes(time_size, videos)
    edges = message[:, : -(-table // LANES) * LANES]
    lane = lax.broadcasted_iota(jnp.int32, edges.shape, 1)
    within = lane % EDGE
    place = (lane // EDGE) * frames + within + jnp.where(within < EDGE // 2, 0, frames - EDGE)
    col_ids = video_ids(video_ref, place, lane < table)
    refined = refine(
        edges, place, col_ids, clip_ref, one_ref, bias_one_ref, two_ref, bias_two_ref
    )
    outer_ids = jnp.where((within < 2) | (within >= EDGE - 2), col_ids, -1)
    first_lane = table % LANES
    best = video_best(refined, outer_ids, videos, first_lane)
    best = jnp.maximum(best, message[:, lanes - LANES :])
    row = lax.broadcasted_iota(jnp.int32, best.shape, 0)
    row_ids = ids_at(lambda k: clip_ref[k], clips, row)
    for c in range(clips):
        total = jnp.sum(jnp.where(row_ids == c, best, 0.0), axis=0, keepdims=True)
        scores_ref[0, c : c + 1, :] = (
            total[:, first_lane : first_lane + videos] / clip_ref[c].astype(jnp.float32)
        )


def call(kernel, name, out_shape, arrays, scalars=()):
    in_smem = pl.BlockSpec(memory_space=pltpu.SMEM)
    in_vmem = pl.BlockSpec(memory_space=pltpu.VMEM)
    return pl.pallas_call(
        kernel,
        in_specs=[in_smem] * len(scalars) + [in_vmem] * len(arrays),
        out_specs=in_vmem,
        out_shape=out_shape,
        compiler_params=pltpu.CompilerParams(vmem_limit_bytes=VMEM_LIMIT),
        name=name,
    )(*scalars, *arrays)


def shards(
    queries, index_regions, conv_one, bias_one, conv_two, bias_two, index_lengths, query_lengths
):
    cycle_size = lax.axis_size("blk")
    time_size = lax.axis_size("tm")
    block_rows, regions, depth = queries.shape
    total_rows = block_rows * cycle_size
    index = index_regions[0]
    frames = index.shape[1]
    videos = index_lengths.shape[1]
    odd = lax.axis_index("tm") % 2 == 1
    half = depth // 2
    width = regions * block_rows

    def sent(x, source):
        pairs = []
        for t in range(time_size):
            for b in range(cycle_size):
                found = source(t, b)
                if found is not None and 0 <= found[0] < time_size:
                    pairs.append((found[0] * cycle_size + found[1], t * cycle_size + b))
        return lax.ppermute(x, ("tm", "blk"), pairs)

    def beside(t, b):
        return t ^ 1, b

    flat = jnp.swapaxes(queries, 0, 1).reshape(width, depth)
    scalars = (index_lengths, query_lengths, conv_one, bias_one, conv_two, bias_two)
    if cycle_size == 4:
        first = jnp.where(odd, flat[:, :half], flat[:, half:])
        second = jnp.where(odd, flat[:, half:], flat[:, :half])

        def near(t, b):
            return (t, b ^ 1) if t % 2 == 0 else (t, b ^ 2)

        def far(t, b):
            return (t ^ 1, b ^ 1) if t % 2 == 0 else (t ^ 1, b ^ 2)

        near_first = sent(first, near)
        near_second = sent(second, near)
        own = call(
            own_kernel,
            "own_maxima",
            jax.ShapeDtypeStruct((frames, width), jnp.float32),
            (index, first, second),
        )
        near_first, own = lax.optimization_barrier((near_first, own))
        far_first = sent(near_first, far)
        next_first = sent(near_first, beside)
        next_second = sent(near_second, beside)
        similar = call(
            functools.partial(near_kernel, block_rows, total_rows),
            "near_similarity",
            jax.ShapeDtypeStruct((total_rows, LANES), jnp.float32),
            (index, near_first, near_second, own),
        )
        far_first, similar = lax.optimization_barrier((far_first, similar))
        far_second = sent(far_first, beside)
        products = call(
            half_kernel,
            "half_products",
            jax.ShapeDtypeStruct((regions * frames, 2 * width), jnp.float32),
            (index, next_first, far_first),
        )
        count, pieces = 0, (next_second, far_second, products, similar)
    else:
        every = lax.all_gather(flat, "blk")
        count, pieces = cycle_size, [every[b] for b in range(cycle_size)]
    _, lanes = message_lanes(time_size, videos)
    message = call(
        functools.partial(late_kernel, count, block_rows, total_rows),
        "late_similarity",
        jax.ShapeDtypeStruct((total_rows, lanes), jnp.float32),
        (index, *pieces),
        scalars,
    )
    step = 1
    while step < time_size:
        other = sent(message, lambda t, b: (t ^ step, b))
        if 2 * step < time_size:
            message = jnp.maximum(message, other)
        step *= 2
    return call(
        functools.partial(score_kernel, frames, time_size),
        "clip_scores",
        jax.ShapeDtypeStruct((1, query_lengths.shape[0], videos), jnp.float32),
        (message, other),
        scalars,
    )


def solution(mesh):
    placed = (
        P("blk", None, None),
        P("blk", None, "tm", None),
        P(),
        P(),
        P(),
        P(),
        P("blk", None),
        P(),
    )
    return jax.shard_map(
        shards, mesh=mesh, in_specs=placed, out_specs=P("blk", None, None), check_vma=False
    )
```

```python
import functools
import jax
import jax.numpy as jnp
from jax import lax
from jax.experimental import pallas as pl
from jax.experimental.pallas import tpu as pltpu
from jax.sharding import PartitionSpec as P

very_low = -1000000000.0
LANES = 128
SUBLANES = 8
EDGE = 8
VMEM_LIMIT = 32 * 1024 * 1024


def inner(a, b):
    return lax.dot_general(a, b, (((1,), (1,)), ((), ())), preferred_element_type=jnp.float32)


def stacked(refs):
    return refs[0][...] if len(refs) == 1 else jnp.concatenate([r[...] for r in refs], axis=0)


def products_of(index_ref, parts):
    regions, frames, _ = index_ref.shape
    total = None
    for first, size, refs in parts:
        rows = index_ref[:, :, pl.ds(first, size)].reshape(regions * frames, size)
        products = inner(rows, stacked(refs))
        total = products if total is None else total + products
    return total


def region_maxima(products, regions):
    return jnp.max(products.reshape(regions, -1, products.shape[1]), axis=0)


def region_mean(maxima, blocks, block_rows, regions, total_rows):
    frames, width = maxima.shape
    table = jnp.concatenate([maxima, jnp.zeros((LANES - frames, width), jnp.float32)], axis=0)
    row = lax.broadcasted_iota(jnp.int32, (total_rows, width), 0)
    lane = lax.broadcasted_iota(jnp.int32, (total_rows, width), 1)
    per_block = regions * block_rows
    picked = jnp.zeros((total_rows, width), jnp.bool_)
    for number, block in enumerate(blocks):
        inside = (lane >= number * per_block) & (lane < (number + 1) * per_block)
        picked = picked | (inside & (row == block * block_rows + lane % block_rows))
    picked = picked.astype(jnp.bfloat16)
    total = None
    for _ in range(3):
        piece = table.astype(jnp.bfloat16)
        table = table - piece.astype(jnp.float32)
        summed = inner(picked, piece)
        total = summed if total is None else total + summed
    return total


def rolled(x, step, axis):
    return x if step == 0 else pltpu.roll(x, (-step) % x.shape[axis], axis)


def ids_at(lengths_ref, positions):
    found = jnp.full(positions.shape, -1, jnp.int32)
    start = jnp.zeros(positions.shape, jnp.int32)
    for k in range(lengths_ref.shape[1]):
        found = found + (positions >= start).astype(jnp.int32)
        start = start + jnp.broadcast_to(lengths_ref[0:1, k : k + 1], positions.shape)
    return found


def column_rows(video_ref, place, known, counted):
    ids = jnp.where(known, ids_at(video_ref, place), -1)
    rows = [
        ((rolled(ids, b, 1) == ids) & (ids >= 0) & (rolled(place, b, 1) == place + b)).astype(
            jnp.float32
        )
        for b in (-1, 0, 1)
    ]
    rows.append(jnp.where(counted, ids, -1).astype(jnp.float32))
    slot = lax.broadcasted_iota(jnp.int32, place.shape, 0)
    table = rows[3]
    for k in range(3):
        table = jnp.where(slot == k, rows[k], table)
    return table


def tables_kernel(
    frames, time_size, total_rows, video_ref, clip_ref, one_ref, bias_one_ref, two_ref, bias_two_ref,
    weights_ref, rows_ref, inner_ref, outer_ref, lengths_ref,
):
    channels = one_ref.shape[0]
    spread = (channels, LANES)
    for t in range(9):
        at = t * channels
        weights_ref[at : at + channels] = jnp.broadcast_to(one_ref[:, t : t + 1], spread)
        at = (9 + t) * channels
        weights_ref[at : at + channels] = jnp.broadcast_to(two_ref[:, t : t + 1], spread)
    square = (channels, channels)
    diagonal = lax.broadcasted_iota(jnp.int32, square, 0) == lax.broadcasted_iota(jnp.int32, square, 1)
    bias = jnp.where(diagonal, jnp.broadcast_to(bias_one_ref[0:1, :], square), 0.0)
    at = 18 * channels
    weights_ref[at : at + channels] = jnp.broadcast_to(jnp.sum(bias, axis=1, keepdims=True), spread)
    at = 19 * channels
    weights_ref[at : at + SUBLANES] = jnp.broadcast_to(bias_two_ref[0:1, 0:1], (SUBLANES, LANES))

    row = lax.broadcasted_iota(jnp.int32, (total_rows, LANES), 0)
    row_ids = ids_at(clip_ref, row)
    for k, a in enumerate((-1, 1)):
        same = (rolled(row_ids, a, 0) == row_ids) & (row + a >= 0) & (row + a < total_rows)
        rows_ref[k * total_rows : (k + 1) * total_rows] = same.astype(jnp.float32)
    rows_ref[2 * total_rows :] = row_ids.astype(jnp.float32)
    for c in range(clip_ref.shape[1]):
        lengths_ref[c : c + 1] = jnp.broadcast_to(
            clip_ref[0:1, c : c + 1].astype(jnp.float32), (1, LANES)
        )

    lane = lax.broadcasted_iota(jnp.int32, inner_ref.shape, 1)
    place = lax.axis_index("tm") * frames + lane
    inner_ref[...] = column_rows(
        video_ref, place, lane < frames, (lane >= 2) & (lane < frames - 2)
    )
    lane = lax.broadcasted_iota(jnp.int32, outer_ref.shape, 1)
    within = lane % EDGE
    place = (lane // EDGE) * frames + within + jnp.where(within < EDGE // 2, 0, frames - EDGE)
    outer_ref[...] = column_rows(
        video_ref, place, lane < time_size * EDGE, (within < 2) | (within >= EDGE - 2)
    )


def refine(similar, columns_ref, rows_ref, weights_ref):
    total_rows, _ = similar.shape
    channels = weights_ref.shape[0] // 19
    steps = (-1, 0, 1)
    col_mask = [columns_ref[k : k + 1, :] for k in range(3)]
    row_mask = {}
    for k, a in enumerate((-1, 1)):
        mask = rows_ref[k * total_rows : (k + 1) * total_rows, :]
        row_mask[a] = jnp.concatenate([mask] * (similar.shape[1] // LANES), axis=1)
    across = [rolled(similar, b, 1) * col_mask[b + 1] for b in steps]
    taps = []
    for a in steps:
        for b in steps:
            tap = across[b + 1]
            taps.append(tap if a == 0 else rolled(tap, a, 0) * row_mask[a])
    piece = 2 * SUBLANES
    gathered = [[] for _ in range(9)]

    def weight(kind, c):
        one = weights_ref[kind * channels + c : kind * channels + c + 1, :]
        return jnp.concatenate([one] * (similar.shape[1] // LANES), axis=1)

    for top in range(0, total_rows, piece):
        source = [tap[top : top + piece] for tap in taps]
        sums = [None] * 9
        for c in range(channels):
            hidden = weight(0, c) * source[0] + weight(18, c)
            for t in range(1, 9):
                hidden = hidden + weight(t, c) * source[t]
            hidden = jnp.maximum(hidden, 0.0)
            for t in range(9):
                term = weight(9 + t, c) * hidden
                sums[t] = term if c == 0 else sums[t] + term
        for t in range(9):
            gathered[t].append(sums[t])
    gathered = [jnp.concatenate(parts, axis=0) for parts in gathered]
    refined = weight(19, 0)
    for b in steps:
        column = gathered[3 + b + 1]
        for a in (-1, 1):
            column = column + rolled(gathered[3 * (a + 1) + b + 1], a, 0) * row_mask[a]
        refined = refined + rolled(column, b, 1) * col_mask[b + 1]
    return refined


def video_best(refined, columns_ref, videos, first_lane):
    ids = columns_ref[3:4, :]
    lane = lax.broadcasted_iota(jnp.int32, (refined.shape[0], LANES), 1)
    best = jnp.full(lane.shape, very_low, jnp.float32)
    for v in range(videos):
        top = jnp.max(jnp.where(ids == v, refined, very_low), axis=1, keepdims=True)
        best = jnp.where(lane == first_lane + v, top, best)
    return best


def message_lanes(time_size, videos):
    table = time_size * EDGE
    lanes = -(-(table + videos) // LANES) * LANES
    assert table // LANES == lanes // LANES - 1
    return table, lanes


def halves(depth, layout):
    half = depth // 2
    parity = lax.axis_index("tm") % 2
    sides = (parity, 1 - parity)
    return [(pl.multiple_of(sides[k] * half, LANES), half, refs) for k, refs in layout]


def own_kernel(index_ref, first_ref, second_ref, maxima_ref):
    parts = halves(index_ref.shape[2], ((1, [first_ref]), (0, [second_ref])))
    maxima_ref[...] = region_maxima(products_of(index_ref, parts), index_ref.shape[0])


def near_kernel(
    block_rows, total_rows, index_ref, first_ref, second_ref, own_ref, similar_ref
):
    regions = index_ref.shape[0]
    parts = halves(index_ref.shape[2], ((1, [first_ref]), (0, [second_ref])))
    near = region_maxima(products_of(index_ref, parts), regions)
    block = lax.axis_index("blk")
    parity = lax.axis_index("tm") % 2
    mean_of = functools.partial(
        region_mean, block_rows=block_rows, regions=regions, total_rows=total_rows
    )
    similar_ref[...] = mean_of(own_ref[...], (block,)) + mean_of(near, (block ^ (1 + parity),))


def half_kernel(index_ref, next_ref, far_ref, products_ref):
    parts = halves(index_ref.shape[2], ((0, [next_ref, far_ref]),))
    products_ref[...] = products_of(index_ref, parts)


def late_kernel(
    count, block_rows, total_rows, videos, columns_ref, rows_ref, weights_ref, index_ref, *refs
):
    *refs, message_ref = refs
    regions, frames, depth = index_ref.shape
    time_index = lax.axis_index("tm")
    mean_of = functools.partial(
        region_mean, block_rows=block_rows, regions=regions, total_rows=total_rows
    )
    if count:
        products = products_of(index_ref, ((0, depth, refs),))
        similar = mean_of(region_maxima(products, regions), tuple(range(count)))
    else:
        next_ref, far_ref, products_ref, similar_ref = refs
        parts = halves(depth, ((1, [next_ref, far_ref]),))
        products = products_ref[...] + products_of(index_ref, parts)
        parity = time_index % 2
        block = lax.axis_index("blk")
        blocks = (block ^ (2 - parity), block ^ 3)
        similar = similar_ref[...] + mean_of(region_maxima(products, regions), blocks)
    similar = similar * (1.0 / regions)
    lane = lax.broadcasted_iota(jnp.int32, similar.shape, 1)
    refined = refine(similar, columns_ref, rows_ref, weights_ref)
    table, lanes = message_lanes(lax.axis_size("tm"), videos)
    best = video_best(refined, columns_ref, videos, table % LANES)
    edges = jnp.where(lane < EDGE // 2, similar, rolled(similar, frames - EDGE, 1))
    edges = jnp.where(lane < EDGE, edges, very_low)
    slot = time_index * EDGE
    edges = pltpu.roll(edges, slot % LANES, 1)
    for k in range(lanes // LANES):
        tile = jnp.where(slot // LANES == k, edges, very_low)
        if k == table // LANES:
            tile = jnp.maximum(tile, best)
        message_ref[:, k * LANES : (k + 1) * LANES] = tile


def score_kernel(time_size, videos, columns_ref, rows_ref, weights_ref, lengths_ref, *refs):
    *messages, scores_ref = refs
    message = messages[0][...]
    for other in messages[1:]:
        message = jnp.maximum(message, other[...])
    table, lanes = message_lanes(time_size, videos)
    edges = message[:, : columns_ref.shape[1]]
    total_rows = edges.shape[0]
    refined = refine(edges, columns_ref, rows_ref, weights_ref)
    first_lane = table % LANES
    best = video_best(refined, columns_ref, videos, first_lane)
    best = jnp.maximum(best, message[:, lanes - LANES :])
    row_ids = rows_ref[2 * total_rows :, :]
    for c in range(scores_ref.shape[1]):
        total = jnp.sum(jnp.where(row_ids == c, best, 0.0), axis=0, keepdims=True)
        total = total / lengths_ref[c : c + 1, :]
        scores_ref[0, c : c + 1, :] = total[:, first_lane : first_lane + videos]


def call(kernel, name, out_shape, *arrays):
    place = pl.BlockSpec(memory_space=pltpu.VMEM)
    return pl.pallas_call(
        kernel,
        in_specs=[place] * len(arrays),
        out_specs=jax.tree.map(lambda _: place, out_shape),
        out_shape=out_shape,
        compiler_params=pltpu.CompilerParams(vmem_limit_bytes=VMEM_LIMIT),
        name=name,
    )(*arrays)


def wide(*shape):
    return jax.ShapeDtypeStruct(shape, jnp.float32)


def shards(
    queries, index_regions, conv_one, bias_one, conv_two, bias_two, index_lengths, query_lengths
):
    cycle_size = lax.axis_size("blk")
    time_size = lax.axis_size("tm")
    block_rows, regions, depth = queries.shape
    total_rows = block_rows * cycle_size
    index = index_regions[0]
    frames = index.shape[1]
    videos = index_lengths.shape[1]
    odd = lax.axis_index("tm") % 2 == 1
    half = depth // 2
    width = regions * block_rows

    def sent(x, source):
        pairs = []
        for t in range(time_size):
            for b in range(cycle_size):
                found = source(t, b)
                if found is not None and 0 <= found[0] < time_size:
                    pairs.append((found[0] * cycle_size + found[1], t * cycle_size + b))
        return lax.ppermute(x, ("tm", "blk"), pairs)

    def beside(t, b):
        return t ^ 1, b

    flat = jnp.swapaxes(queries, 0, 1).reshape(width, depth)
    clips = query_lengths.shape[0]
    channels = conv_one.shape[0]
    edge_lanes = -(-time_size * EDGE // LANES) * LANES
    weights, rows, inner_columns, outer_columns, lengths = call(
        functools.partial(tables_kernel, frames, time_size, total_rows),
        "tables",
        (
            wide(19 * channels + SUBLANES, LANES),
            wide(3 * total_rows, LANES),
            wide(SUBLANES, LANES),
            wide(SUBLANES, edge_lanes),
            wide(clips, LANES),
        ),
        index_lengths,
        query_lengths.reshape(1, clips),
        conv_one,
        bias_one.reshape(1, channels),
        conv_two,
        bias_two.reshape(1, 1),
    )
    if cycle_size == 4:
        first = jnp.where(odd, flat[:, :half], flat[:, half:])
        second = jnp.where(odd, flat[:, half:], flat[:, :half])

        def near(t, b):
            return (t, b ^ 1) if t % 2 == 0 else (t, b ^ 2)

        def far(t, b):
            return (t ^ 1, b ^ 1) if t % 2 == 0 else (t ^ 1, b ^ 2)

        near_first = sent(first, near)
        near_second = sent(second, near)
        own = call(own_kernel, "own_maxima", wide(frames, width), index, first, second)
        near_first, own, weights = lax.optimization_barrier((near_first, own, weights))
        far_first = sent(near_first, far)
        next_first = sent(near_first, beside)
        next_second = sent(near_second, beside)
        similar = call(
            functools.partial(near_kernel, block_rows, total_rows),
            "near_similarity",
            wide(total_rows, LANES),
            index, near_first, near_second, own,
        )
        far_first, similar = lax.optimization_barrier((far_first, similar))
        far_second = sent(far_first, beside)
        products = call(
            half_kernel,
            "half_products",
            wide(regions * frames, 2 * width),
            index, next_first, far_first,
        )
        count, pieces = 0, (next_second, far_second, products, similar)
    else:
        every = lax.all_gather(flat, "blk")
        count, pieces = cycle_size, [every[b] for b in range(cycle_size)]
    _, lanes = message_lanes(time_size, videos)
    message = call(
        functools.partial(late_kernel, count, block_rows, total_rows, videos),
        "late_similarity",
        wide(total_rows, lanes),
        inner_columns, rows, weights, index, *pieces,
    )
    step = 1
    while step < time_size:
        other = sent(message, lambda t, b: (t ^ step, b))
        if 2 * step < time_size:
            message = jnp.maximum(message, other)
        step *= 2
    return call(
        functools.partial(score_kernel, time_size, videos),
        "clip_scores",
        wide(1, clips, videos),
        outer_columns, rows, weights, lengths, message, other,
    )


def solution(mesh):
    placed = (
        P("blk", None, None),
        P("blk", None, "tm", None),
        P(),
        P(),
        P(),
        P(),
        P("blk", None),
        P(),
    )
    return jax.shard_map(
        shards, mesh=mesh, in_specs=placed, out_specs=P("blk", None, None), check_vma=False
    )
```

```python
import functools
import jax
import jax.numpy as jnp
from jax import lax
from jax.experimental import pallas as pl
from jax.experimental.pallas import tpu as pltpu
from jax.sharding import PartitionSpec as P

very_low = -1000000000.0
LANES = 128
SUBLANES = 8
EDGE = 8
QUARTER = 32
VMEM_LIMIT = 32 * 1024 * 1024


def inner(a, b):
    return lax.dot_general(a, b, (((1,), (1,)), ((), ())), preferred_element_type=jnp.float32)


def stacked(refs):
    return refs[0][...] if len(refs) == 1 else jnp.concatenate([r[...] for r in refs], axis=0)


def products_of(index_ref, parts):
    regions, frames, _ = index_ref.shape
    total = None
    for first, size, refs in parts:
        rows = index_ref[:, :, pl.ds(first, size)].reshape(regions * frames, size)
        products = inner(rows, stacked(refs))
        total = products if total is None else total + products
    return total


def region_maxima(products, regions):
    return jnp.max(products.reshape(regions, -1, products.shape[1]), axis=0)


def region_mean(maxima, blocks, block_rows, regions, total_rows):
    frames, width = maxima.shape
    table = jnp.concatenate([maxima, jnp.zeros((LANES - frames, width), jnp.float32)], axis=0)
    row = lax.broadcasted_iota(jnp.int32, (total_rows, width), 0)
    lane = lax.broadcasted_iota(jnp.int32, (total_rows, width), 1)
    per_block = regions * block_rows
    picked = jnp.zeros((total_rows, width), jnp.bool_)
    for number, block in enumerate(blocks):
        inside = (lane >= number * per_block) & (lane < (number + 1) * per_block)
        picked = picked | (inside & (row == block * block_rows + lane % block_rows))
    picked = picked.astype(jnp.bfloat16)
    total = None
    for _ in range(3):
        piece = table.astype(jnp.bfloat16)
        table = table - piece.astype(jnp.float32)
        summed = inner(picked, piece)
        total = summed if total is None else total + summed
    return total


def rolled(x, step, axis):
    return x if step == 0 else pltpu.roll(x, (-step) % x.shape[axis], axis)


def ids_at(lengths_ref, positions):
    found = jnp.full(positions.shape, -1, jnp.int32)
    start = jnp.zeros(positions.shape, jnp.int32)
    for k in range(lengths_ref.shape[1]):
        found = found + (positions >= start).astype(jnp.int32)
        start = start + jnp.broadcast_to(lengths_ref[0:1, k : k + 1], positions.shape)
    return found


def column_rows(video_ref, place, known, counted):
    ids = jnp.where(known, ids_at(video_ref, place), -1)
    rows = [
        ((rolled(ids, b, 1) == ids) & (ids >= 0) & (rolled(place, b, 1) == place + b)).astype(
            jnp.float32
        )
        for b in (-1, 0, 1)
    ]
    rows.append(jnp.where(counted, ids, -1).astype(jnp.float32))
    slot = lax.broadcasted_iota(jnp.int32, place.shape, 0)
    table = rows[3]
    for k in range(3):
        table = jnp.where(slot == k, rows[k], table)
    return table


def tables_kernel(
    frames, time_size, total_rows, video_ref, clip_ref, one_ref, bias_one_ref, two_ref, bias_two_ref,
    weights_ref, rows_ref, inner_ref, outer_ref, lengths_ref,
):
    channels = one_ref.shape[0]
    spread = (channels, LANES)
    for t in range(9):
        at = t * channels
        weights_ref[at : at + channels] = jnp.broadcast_to(one_ref[:, t : t + 1], spread)
        at = (9 + t) * channels
        weights_ref[at : at + channels] = jnp.broadcast_to(two_ref[:, t : t + 1], spread)
    square = (channels, channels)
    diagonal = lax.broadcasted_iota(jnp.int32, square, 0) == lax.broadcasted_iota(jnp.int32, square, 1)
    bias = jnp.where(diagonal, jnp.broadcast_to(bias_one_ref[0:1, :], square), 0.0)
    at = 18 * channels
    weights_ref[at : at + channels] = jnp.broadcast_to(jnp.sum(bias, axis=1, keepdims=True), spread)
    at = 19 * channels
    weights_ref[at : at + SUBLANES] = jnp.broadcast_to(bias_two_ref[0:1, 0:1], (SUBLANES, LANES))

    row = lax.broadcasted_iota(jnp.int32, (total_rows, LANES), 0)
    row_ids = ids_at(clip_ref, row)
    for k, a in enumerate((-1, 1)):
        same = (rolled(row_ids, a, 0) == row_ids) & (row + a >= 0) & (row + a < total_rows)
        rows_ref[k * total_rows : (k + 1) * total_rows] = same.astype(jnp.float32)
    rows_ref[2 * total_rows :] = row_ids.astype(jnp.float32)
    for c in range(clip_ref.shape[1]):
        lengths_ref[c : c + 1] = jnp.broadcast_to(
            clip_ref[0:1, c : c + 1].astype(jnp.float32), (1, LANES)
        )

    lane = lax.broadcasted_iota(jnp.int32, inner_ref.shape, 1)
    place = lax.axis_index("tm") * frames + lane
    inner_ref[...] = column_rows(
        video_ref, place, lane < frames, (lane >= 2) & (lane < frames - 2)
    )
    lane = lax.broadcasted_iota(jnp.int32, outer_ref.shape, 1)
    within = lane % EDGE
    place = (lane // EDGE) * frames + within + jnp.where(within < EDGE // 2, 0, frames - EDGE)
    outer_ref[...] = column_rows(
        video_ref, place, lane < time_size * EDGE, (within < 2) | (within >= EDGE - 2)
    )


def refine(similar, columns_ref, rows_ref, weights_ref):
    total_rows, _ = similar.shape
    channels = weights_ref.shape[0] // 19
    steps = (-1, 0, 1)
    col_mask = [columns_ref[k : k + 1, :] for k in range(3)]
    row_mask = {}
    for k, a in enumerate((-1, 1)):
        mask = rows_ref[k * total_rows : (k + 1) * total_rows, :]
        row_mask[a] = jnp.concatenate([mask] * (similar.shape[1] // LANES), axis=1)
    across = [rolled(similar, b, 1) * col_mask[b + 1] for b in steps]
    taps = []
    for a in steps:
        for b in steps:
            tap = across[b + 1]
            taps.append(tap if a == 0 else rolled(tap, a, 0) * row_mask[a])
    piece = 2 * SUBLANES
    gathered = [[] for _ in range(9)]

    def weight(kind, c):
        one = weights_ref[kind * channels + c : kind * channels + c + 1, :]
        return jnp.concatenate([one] * (similar.shape[1] // LANES), axis=1)

    for top in range(0, total_rows, piece):
        source = [tap[top : top + piece] for tap in taps]
        sums = [None] * 9
        for c in range(channels):
            hidden = weight(0, c) * source[0] + weight(18, c)
            for t in range(1, 9):
                hidden = hidden + weight(t, c) * source[t]
            hidden = jnp.maximum(hidden, 0.0)
            for t in range(9):
                term = weight(9 + t, c) * hidden
                sums[t] = term if c == 0 else sums[t] + term
        for t in range(9):
            gathered[t].append(sums[t])
    gathered = [jnp.concatenate(parts, axis=0) for parts in gathered]
    refined = weight(19, 0)
    for b in steps:
        column = gathered[3 + b + 1]
        for a in (-1, 1):
            column = column + rolled(gathered[3 * (a + 1) + b + 1], a, 0) * row_mask[a]
        refined = refined + rolled(column, b, 1) * col_mask[b + 1]
    return refined


def video_best(refined, columns_ref, videos, first_lane):
    ids = columns_ref[3:4, :]
    lane = lax.broadcasted_iota(jnp.int32, (refined.shape[0], LANES), 1)
    best = jnp.full(lane.shape, very_low, jnp.float32)
    for v in range(videos):
        top = jnp.max(jnp.where(ids == v, refined, very_low), axis=1, keepdims=True)
        best = jnp.where(lane == first_lane + v, top, best)
    return best


def message_lanes(time_size, videos):
    table = time_size * EDGE
    lanes = -(-(table + videos) // LANES) * LANES
    assert table // LANES == lanes // LANES - 1
    return table, lanes


def halves(depth, layout):
    half = depth // 2
    parity = lax.axis_index("tm") % 2
    sides = (parity, 1 - parity)
    return [(pl.multiple_of(sides[k] * half, LANES), half, refs) for k, refs in layout]


def own_kernel(index_ref, first_ref, second_ref, maxima_ref):
    parts = halves(index_ref.shape[2], ((1, [first_ref]), (0, [second_ref])))
    maxima_ref[...] = region_maxima(products_of(index_ref, parts), index_ref.shape[0])


def near_kernel(
    block_rows, total_rows, index_ref, first_ref, second_ref, own_ref, similar_ref
):
    regions = index_ref.shape[0]
    parts = halves(index_ref.shape[2], ((1, [first_ref]), (0, [second_ref])))
    near = region_maxima(products_of(index_ref, parts), regions)
    block = lax.axis_index("blk")
    parity = lax.axis_index("tm") % 2
    mean_of = functools.partial(
        region_mean, block_rows=block_rows, regions=regions, total_rows=total_rows
    )
    similar_ref[...] = mean_of(own_ref[...], (block,)) + mean_of(near, (block ^ (2 - parity),))


def half_kernel(index_ref, next_ref, far_ref, products_ref):
    parts = halves(index_ref.shape[2], ((0, [next_ref, far_ref]),))
    products_ref[...] = products_of(index_ref, parts)


def late_kernel(
    count, block_rows, total_rows, videos, packed,
    columns_ref, rows_ref, weights_ref, index_ref, *refs,
):
    *refs, message_ref = refs
    regions, frames, depth = index_ref.shape
    time_index = lax.axis_index("tm")
    mean_of = functools.partial(
        region_mean, block_rows=block_rows, regions=regions, total_rows=total_rows
    )
    if count:
        products = products_of(index_ref, ((0, depth, refs),))
        similar = mean_of(region_maxima(products, regions), tuple(range(count)))
    else:
        next_ref, far_ref, products_ref, similar_ref = refs
        parts = halves(depth, ((1, [next_ref, far_ref]),))
        products = products_ref[...] + products_of(index_ref, parts)
        parity = time_index % 2
        block = lax.axis_index("blk")
        blocks = (block ^ (1 + parity), block ^ 3)
        similar = similar_ref[...] + mean_of(region_maxima(products, regions), blocks)
    similar = similar * (1.0 / regions)
    lane = lax.broadcasted_iota(jnp.int32, similar.shape, 1)
    refined = refine(similar, columns_ref, rows_ref, weights_ref)
    edges = jnp.where(lane < EDGE // 2, similar, rolled(similar, frames - EDGE, 1))
    edges = jnp.where(lane < EDGE, edges, very_low)
    if packed:
        best = video_best(refined, columns_ref, videos, 0)
        whole = jnp.maximum(best, pltpu.roll(edges, EDGE * (1 + time_index % 2), 1))
        lane = lax.broadcasted_iota(jnp.int32, (SUBLANES, LANES), 1)
        message = whole[:SUBLANES]
        for g in range(1, 4):
            part = pltpu.roll(whole[g * SUBLANES : (g + 1) * SUBLANES], g * QUARTER, 1)
            message = jnp.where(lane < g * QUARTER, message, part)
        message_ref[...] = message
        return
    table, lanes = message_lanes(lax.axis_size("tm"), videos)
    best = video_best(refined, columns_ref, videos, table % LANES)
    slot = time_index * EDGE
    edges = pltpu.roll(edges, slot % LANES, 1)
    for k in range(lanes // LANES):
        tile = jnp.where(slot // LANES == k, edges, very_low)
        if k == table // LANES:
            tile = jnp.maximum(tile, best)
        message_ref[:, k * LANES : (k + 1) * LANES] = tile


def unpacked(pairs, table_lane):
    together = functools.reduce(jnp.maximum, pairs)
    lane = lax.broadcasted_iota(jnp.int32, together.shape, 1)
    mine = lax.axis_index("tm") // 2
    edges = []
    table = []
    for g in range(4):
        found = jnp.zeros_like(together)
        for k, pair in enumerate(pairs):
            target = 2 * EDGE * (mine ^ k)
            moved = pltpu.roll(pair, (target + LANES - g * QUARTER - EDGE) % LANES, 1)
            found = jnp.where(lane // (2 * EDGE) == mine ^ k, moved, found)
        edges.append(found)
        table.append(rolled(together, g * QUARTER - table_lane, 1))
    return jnp.concatenate(edges, axis=0), jnp.concatenate(table, axis=0)


def score_kernel(
    time_size, videos, packed, columns_ref, rows_ref, weights_ref, lengths_ref, *refs
):
    *messages, scores_ref = refs
    messages = [message[...] for message in messages]
    if packed:
        messages = [m[k : k + SUBLANES] for m in messages for k in (0, SUBLANES)]
    first, lanes = message_lanes(time_size, videos)
    first_lane = first % LANES
    if packed:
        edges, table = unpacked(messages, first_lane)
    else:
        message = functools.reduce(jnp.maximum, messages)
        edges, table = message[:, : columns_ref.shape[1]], message[:, lanes - LANES :]
    total_rows = edges.shape[0]
    refined = refine(edges, columns_ref, rows_ref, weights_ref)
    best = jnp.maximum(table, video_best(refined, columns_ref, videos, first_lane))
    row_ids = rows_ref[2 * total_rows :, :]
    for c in range(scores_ref.shape[1]):
        total = jnp.sum(jnp.where(row_ids == c, best, 0.0), axis=0, keepdims=True)
        total = total / lengths_ref[c : c + 1, :]
        scores_ref[0, c : c + 1, :] = total[:, first_lane : first_lane + videos]


def call(kernel, name, out_shape, *arrays):
    place = pl.BlockSpec(memory_space=pltpu.VMEM)
    return pl.pallas_call(
        kernel,
        in_specs=[place] * len(arrays),
        out_specs=jax.tree.map(lambda _: place, out_shape),
        out_shape=out_shape,
        compiler_params=pltpu.CompilerParams(vmem_limit_bytes=VMEM_LIMIT),
        name=name,
    )(*arrays)


def wide(*shape):
    return jax.ShapeDtypeStruct(shape, jnp.float32)


def shards(
    queries, index_regions, conv_one, bias_one, conv_two, bias_two, index_lengths, query_lengths
):
    cycle_size = lax.axis_size("blk")
    time_size = lax.axis_size("tm")
    block_rows, regions, depth = queries.shape
    total_rows = block_rows * cycle_size
    index = index_regions[0]
    frames = index.shape[1]
    videos = index_lengths.shape[1]
    odd = lax.axis_index("tm") % 2 == 1
    half = depth // 2
    width = regions * block_rows

    def sent(x, source):
        pairs = []
        for t in range(time_size):
            for b in range(cycle_size):
                found = source(t, b)
                if found is not None and 0 <= found[0] < time_size:
                    pairs.append((found[0] * cycle_size + found[1], t * cycle_size + b))
        return lax.ppermute(x, ("tm", "blk"), pairs)

    def beside(t, b):
        return t ^ 1, b

    flat = jnp.swapaxes(queries, 0, 1).reshape(width, depth)
    clips = query_lengths.shape[0]
    channels = conv_one.shape[0]
    edge_lanes = -(-time_size * EDGE // LANES) * LANES
    weights, rows, inner_columns, outer_columns, lengths = call(
        functools.partial(tables_kernel, frames, time_size, total_rows),
        "tables",
        (
            wide(19 * channels + SUBLANES, LANES),
            wide(3 * total_rows, LANES),
            wide(SUBLANES, LANES),
            wide(SUBLANES, edge_lanes),
            wide(clips, LANES),
        ),
        index_lengths,
        query_lengths.reshape(1, clips),
        conv_one,
        bias_one.reshape(1, channels),
        conv_two,
        bias_two.reshape(1, 1),
    )
    if cycle_size == 4:
        first = jnp.where(odd, flat[:, :half], flat[:, half:])
        second = jnp.where(odd, flat[:, half:], flat[:, :half])

        def near(t, b):
            return (t, b ^ 2) if t % 2 == 0 else (t, b ^ 1)

        def far(t, b):
            return (t ^ 1, b ^ 2) if t % 2 == 0 else (t ^ 1, b ^ 1)

        near_first = sent(first, near)
        near_second = sent(second, near)
        own = call(own_kernel, "own_maxima", wide(frames, width), index, first, second)
        near_first, own = lax.optimization_barrier((near_first, own))
        far_first = sent(near_first, far)
        next_first = sent(near_first, beside)
        near_second, weights = lax.optimization_barrier((near_second, weights))
        next_second = sent(near_second, beside)
        similar = call(
            functools.partial(near_kernel, block_rows, total_rows),
            "near_similarity",
            wide(total_rows, LANES),
            index, near_first, near_second, own,
        )
        far_first, similar = lax.optimization_barrier((far_first, similar))
        far_second = sent(far_first, beside)
        products = call(
            half_kernel,
            "half_products",
            wide(regions * frames, 2 * width),
            index, next_first, far_first,
        )
        count, pieces = 0, (next_second, far_second, products, similar)
    else:
        every = lax.all_gather(flat, "blk")
        count, pieces = cycle_size, [every[b] for b in range(cycle_size)]
    packed = time_size == 8 and total_rows == 4 * SUBLANES and videos <= EDGE
    shape = (SUBLANES, LANES) if packed else (total_rows, message_lanes(time_size, videos)[1])
    message = call(
        functools.partial(late_kernel, count, block_rows, total_rows, videos, packed),
        "late_similarity",
        wide(*shape),
        inner_columns, rows, weights, index, *pieces,
    )

    def swapped(step):
        return sent(message, lambda t, b: (t ^ step, b))

    if packed:
        message = jnp.maximum(message, swapped(1))
        message = jnp.concatenate([message, swapped(2)])
        messages = [message, swapped(4)]
    else:
        step = 1
        while step < time_size:
            messages = [message, swapped(step)]
            message = jnp.maximum(*messages)
            step *= 2
    return call(
        functools.partial(score_kernel, time_size, videos, packed),
        "clip_scores",
        wide(1, clips, videos),
        outer_columns, rows, weights, lengths, *messages,
    )


def solution(mesh):
    placed = (
        P("blk", None, None),
        P("blk", None, "tm", None),
        P(),
        P(),
        P(),
        P(),
        P("blk", None),
        P(),
    )
    return jax.shard_map(
        shards, mesh=mesh, in_specs=placed, out_specs=P("blk", None, None), check_vma=False
    )
```

```python
import functools
import jax
import jax.numpy as jnp
from jax import lax
from jax.experimental import pallas as pl
from jax.experimental.pallas import tpu as pltpu
from jax.sharding import PartitionSpec as P

very_low = -1000000000.0
LANES = 128
SUBLANES = 8
EDGE = 8
QUARTER = 32
VMEM_LIMIT = 32 * 1024 * 1024


def inner(a, b):
    return lax.dot_general(a, b, (((1,), (1,)), ((), ())), preferred_element_type=jnp.float32)


def stacked(refs):
    return refs[0][...] if len(refs) == 1 else jnp.concatenate([r[...] for r in refs], axis=0)


def products_of(index_ref, parts):
    regions, frames, _ = index_ref.shape
    total = None
    for first, size, refs in parts:
        rows = index_ref[:, :, pl.ds(first, size)].reshape(regions * frames, size)
        products = inner(rows, stacked(refs))
        total = products if total is None else total + products
    return total


def region_maxima(products, regions):
    return jnp.max(products.reshape(regions, -1, products.shape[1]), axis=0)


def region_mean(maxima, blocks, block_rows, regions, total_rows):
    frames, width = maxima.shape
    table = jnp.concatenate([maxima, jnp.zeros((LANES - frames, width), jnp.float32)], axis=0)
    row = lax.broadcasted_iota(jnp.int32, (total_rows, width), 0)
    lane = lax.broadcasted_iota(jnp.int32, (total_rows, width), 1)
    per_block = regions * block_rows
    picked = jnp.zeros((total_rows, width), jnp.bool_)
    for number, block in enumerate(blocks):
        inside = (lane >= number * per_block) & (lane < (number + 1) * per_block)
        picked = picked | (inside & (row == block * block_rows + lane % block_rows))
    picked = picked.astype(jnp.bfloat16)
    total = None
    for _ in range(3):
        piece = table.astype(jnp.bfloat16)
        table = table - piece.astype(jnp.float32)
        summed = inner(picked, piece)
        total = summed if total is None else total + summed
    return total


def rolled(x, step, axis):
    return x if step == 0 else pltpu.roll(x, (-step) % x.shape[axis], axis)


def ids_at(lengths_ref, positions):
    found = jnp.full(positions.shape, -1, jnp.int32)
    start = jnp.zeros(positions.shape, jnp.int32)
    for k in range(lengths_ref.shape[1]):
        found = found + (positions >= start).astype(jnp.int32)
        start = start + jnp.broadcast_to(lengths_ref[0:1, k : k + 1], positions.shape)
    return found


def column_rows(video_ref, place, known, counted):
    ids = jnp.where(known, ids_at(video_ref, place), -1)
    rows = [
        ((rolled(ids, b, 1) == ids) & (ids >= 0) & (rolled(place, b, 1) == place + b)).astype(
            jnp.float32
        )
        for b in (-1, 0, 1)
    ]
    rows.append(jnp.where(counted, ids, -1).astype(jnp.float32))
    slot = lax.broadcasted_iota(jnp.int32, place.shape, 0)
    table = rows[3]
    for k in range(3):
        table = jnp.where(slot == k, rows[k], table)
    return table


def tables_kernel(
    frames, time_size, total_rows, video_ref, clip_ref, one_ref, bias_one_ref, two_ref, bias_two_ref,
    weights_ref, rows_ref, inner_ref, outer_ref, lengths_ref,
):
    channels = one_ref.shape[0]
    spread = (channels, LANES)
    for t in range(9):
        at = t * channels
        weights_ref[at : at + channels] = jnp.broadcast_to(one_ref[:, t : t + 1], spread)
        at = (9 + t) * channels
        weights_ref[at : at + channels] = jnp.broadcast_to(two_ref[:, t : t + 1], spread)
    square = (channels, channels)
    diagonal = lax.broadcasted_iota(jnp.int32, square, 0) == lax.broadcasted_iota(jnp.int32, square, 1)
    bias = jnp.where(diagonal, jnp.broadcast_to(bias_one_ref[0:1, :], square), 0.0)
    at = 18 * channels
    weights_ref[at : at + channels] = jnp.broadcast_to(jnp.sum(bias, axis=1, keepdims=True), spread)
    at = 19 * channels
    weights_ref[at : at + SUBLANES] = jnp.broadcast_to(bias_two_ref[0:1, 0:1], (SUBLANES, LANES))

    row = lax.broadcasted_iota(jnp.int32, (total_rows, LANES), 0)
    row_ids = ids_at(clip_ref, row)
    for k, a in enumerate((-1, 1)):
        same = (rolled(row_ids, a, 0) == row_ids) & (row + a >= 0) & (row + a < total_rows)
        rows_ref[k * total_rows : (k + 1) * total_rows] = same.astype(jnp.float32)
    rows_ref[2 * total_rows :] = row_ids.astype(jnp.float32)
    for c in range(clip_ref.shape[1]):
        lengths_ref[c : c + 1] = jnp.broadcast_to(
            clip_ref[0:1, c : c + 1].astype(jnp.float32), (1, LANES)
        )

    lane = lax.broadcasted_iota(jnp.int32, inner_ref.shape, 1)
    place = lax.axis_index("tm") * frames + lane
    inner_ref[...] = column_rows(
        video_ref, place, lane < frames, (lane >= 2) & (lane < frames - 2)
    )
    lane = lax.broadcasted_iota(jnp.int32, outer_ref.shape, 1)
    within = lane % EDGE
    place = (lane // EDGE) * frames + within + jnp.where(within < EDGE // 2, 0, frames - EDGE)
    outer_ref[...] = column_rows(
        video_ref, place, lane < time_size * EDGE, (within < 2) | (within >= EDGE - 2)
    )


def refine(similar, columns_ref, rows_ref, weights_ref):
    total_rows, _ = similar.shape
    channels = weights_ref.shape[0] // 19
    steps = (-1, 0, 1)
    col_mask = [columns_ref[k : k + 1, :] for k in range(3)]
    row_mask = {}
    for k, a in enumerate((-1, 1)):
        mask = rows_ref[k * total_rows : (k + 1) * total_rows, :]
        row_mask[a] = jnp.concatenate([mask] * (similar.shape[1] // LANES), axis=1)
    across = [rolled(similar, b, 1) * col_mask[b + 1] for b in steps]
    taps = []
    for a in steps:
        for b in steps:
            tap = across[b + 1]
            taps.append(tap if a == 0 else rolled(tap, a, 0) * row_mask[a])
    piece = 2 * SUBLANES
    gathered = [[] for _ in range(9)]

    def weight(kind, c):
        one = weights_ref[kind * channels + c : kind * channels + c + 1, :]
        return jnp.concatenate([one] * (similar.shape[1] // LANES), axis=1)

    for top in range(0, total_rows, piece):
        source = [tap[top : top + piece] for tap in taps]
        sums = [None] * 9
        for c in range(channels):
            hidden = weight(0, c) * source[0] + weight(18, c)
            for t in range(1, 9):
                hidden = hidden + weight(t, c) * source[t]
            hidden = jnp.maximum(hidden, 0.0)
            for t in range(9):
                term = weight(9 + t, c) * hidden
                sums[t] = term if c == 0 else sums[t] + term
        for t in range(9):
            gathered[t].append(sums[t])
    gathered = [jnp.concatenate(parts, axis=0) for parts in gathered]
    refined = weight(19, 0)
    for b in steps:
        column = gathered[3 + b + 1]
        for a in (-1, 1):
            column = column + rolled(gathered[3 * (a + 1) + b + 1], a, 0) * row_mask[a]
        refined = refined + rolled(column, b, 1) * col_mask[b + 1]
    return refined


def video_best(refined, columns_ref, videos, first_lane):
    ids = columns_ref[3:4, :]
    lane = lax.broadcasted_iota(jnp.int32, (refined.shape[0], LANES), 1)
    best = jnp.full(lane.shape, very_low, jnp.float32)
    for v in range(videos):
        top = jnp.max(jnp.where(ids == v, refined, very_low), axis=1, keepdims=True)
        best = jnp.where(lane == first_lane + v, top, best)
    return best


def message_lanes(time_size, videos):
    table = time_size * EDGE
    lanes = -(-(table + videos) // LANES) * LANES
    assert table // LANES == lanes // LANES - 1
    return table, lanes


def halves(depth, layout):
    half = depth // 2
    parity = lax.axis_index("tm") % 2
    sides = (parity, 1 - parity)
    return [(pl.multiple_of(sides[k] * half, LANES), half, refs) for k, refs in layout]


def own_kernel(index_ref, first_ref, second_ref, maxima_ref):
    parts = halves(index_ref.shape[2], ((1, [first_ref]), (0, [second_ref])))
    maxima_ref[...] = region_maxima(products_of(index_ref, parts), index_ref.shape[0])


def near_kernel(
    block_rows, total_rows, index_ref, first_ref, second_ref, own_ref, similar_ref
):
    regions = index_ref.shape[0]
    parts = halves(index_ref.shape[2], ((1, [first_ref]), (0, [second_ref])))
    near = region_maxima(products_of(index_ref, parts), regions)
    block = lax.axis_index("blk")
    parity = lax.axis_index("tm") % 2
    mean_of = functools.partial(
        region_mean, block_rows=block_rows, regions=regions, total_rows=total_rows
    )
    similar_ref[...] = mean_of(own_ref[...], (block,)) + mean_of(near, (block ^ (2 - parity),))


def half_kernel(index_ref, next_ref, far_ref, products_ref):
    parts = halves(index_ref.shape[2], ((0, [next_ref, far_ref]),))
    products_ref[...] = products_of(index_ref, parts)


def late_kernel(
    count, block_rows, total_rows, videos, packed,
    columns_ref, rows_ref, weights_ref, index_ref, *refs,
):
    *refs, message_ref = refs
    regions, frames, depth = index_ref.shape
    time_index = lax.axis_index("tm")
    mean_of = functools.partial(
        region_mean, block_rows=block_rows, regions=regions, total_rows=total_rows
    )
    if count:
        products = products_of(index_ref, ((0, depth, refs),))
        similar = mean_of(region_maxima(products, regions), tuple(range(count)))
    else:
        next_ref, far_ref, products_ref, similar_ref = refs
        parts = halves(depth, ((1, [next_ref, far_ref]),))
        products = products_ref[...] + products_of(index_ref, parts)
        parity = time_index % 2
        block = lax.axis_index("blk")
        blocks = (block ^ (1 + parity), block ^ 3)
        similar = similar_ref[...] + mean_of(region_maxima(products, regions), blocks)
    similar = similar * (1.0 / regions)
    lane = lax.broadcasted_iota(jnp.int32, similar.shape, 1)
    refined = refine(similar, columns_ref, rows_ref, weights_ref)
    edges = jnp.where(lane < EDGE // 2, similar, rolled(similar, frames - EDGE, 1))
    edges = jnp.where(lane < EDGE, edges, very_low)
    if packed:
        best = video_best(refined, columns_ref, videos, 0)
        whole = jnp.maximum(best, pltpu.roll(edges, EDGE * (1 + time_index % 2), 1))
        lane = lax.broadcasted_iota(jnp.int32, (SUBLANES, LANES), 1)
        message = whole[:SUBLANES]
        for g in range(1, 4):
            part = pltpu.roll(whole[g * SUBLANES : (g + 1) * SUBLANES], g * QUARTER, 1)
            message = jnp.where(lane < g * QUARTER, message, part)
        message_ref[...] = message
        return
    table, lanes = message_lanes(lax.axis_size("tm"), videos)
    best = video_best(refined, columns_ref, videos, table % LANES)
    slot = time_index * EDGE
    edges = pltpu.roll(edges, slot % LANES, 1)
    for k in range(lanes // LANES):
        tile = jnp.where(slot // LANES == k, edges, very_low)
        if k == table // LANES:
            tile = jnp.maximum(tile, best)
        message_ref[:, k * LANES : (k + 1) * LANES] = tile


def unpacked(pairs, table_lane):
    together = functools.reduce(jnp.maximum, pairs)
    lane = lax.broadcasted_iota(jnp.int32, together.shape, 1)
    mine = lax.axis_index("tm") // 2
    edges = []
    table = []
    for g in range(4):
        found = jnp.zeros_like(together)
        for k, pair in enumerate(pairs):
            target = 2 * EDGE * (mine ^ k)
            moved = pltpu.roll(pair, (target + LANES - g * QUARTER - EDGE) % LANES, 1)
            found = jnp.where(lane // (2 * EDGE) == mine ^ k, moved, found)
        edges.append(found)
        table.append(rolled(together, g * QUARTER - table_lane, 1))
    return jnp.concatenate(edges, axis=0), jnp.concatenate(table, axis=0)


def score_kernel(
    time_size, videos, packed, columns_ref, rows_ref, weights_ref, lengths_ref, *refs
):
    *messages, scores_ref = refs
    messages = [message[...] for message in messages]
    if packed:
        messages = [m[k : k + SUBLANES] for m in messages for k in (0, SUBLANES)]
    first, lanes = message_lanes(time_size, videos)
    first_lane = first % LANES
    if packed:
        edges, table = unpacked(messages, first_lane)
    else:
        message = functools.reduce(jnp.maximum, messages)
        edges, table = message[:, : columns_ref.shape[1]], message[:, lanes - LANES :]
    total_rows = edges.shape[0]
    refined = refine(edges, columns_ref, rows_ref, weights_ref)
    best = jnp.maximum(table, video_best(refined, columns_ref, videos, first_lane))
    row_ids = rows_ref[2 * total_rows :, :]
    for c in range(scores_ref.shape[1]):
        total = jnp.sum(jnp.where(row_ids == c, best, 0.0), axis=0, keepdims=True)
        total = total / lengths_ref[c : c + 1, :]
        scores_ref[0, c : c + 1, :] = total[:, first_lane : first_lane + videos]


def call(kernel, name, out_shape, *arrays):
    place = pl.BlockSpec(memory_space=pltpu.VMEM)
    return pl.pallas_call(
        kernel,
        in_specs=[place] * len(arrays),
        out_specs=jax.tree.map(lambda _: place, out_shape),
        out_shape=out_shape,
        compiler_params=pltpu.CompilerParams(vmem_limit_bytes=VMEM_LIMIT),
        name=name,
    )(*arrays)


def wide(*shape):
    return jax.ShapeDtypeStruct(shape, jnp.float32)


def shards(
    queries, index_regions, conv_one, bias_one, conv_two, bias_two, index_lengths, query_lengths
):
    cycle_size = lax.axis_size("blk")
    time_size = lax.axis_size("tm")
    block_rows, regions, depth = queries.shape
    total_rows = block_rows * cycle_size
    index = index_regions[0]
    frames = index.shape[1]
    videos = index_lengths.shape[1]
    odd = lax.axis_index("tm") % 2 == 1
    half = depth // 2
    width = regions * block_rows

    def sent(x, source):
        pairs = []
        for t in range(time_size):
            for b in range(cycle_size):
                found = source(t, b)
                if found is not None and 0 <= found[0] < time_size:
                    pairs.append((found[0] * cycle_size + found[1], t * cycle_size + b))
        return lax.ppermute(x, ("tm", "blk"), pairs)

    def beside(t, b):
        return t ^ 1, b

    flat = jnp.swapaxes(queries, 0, 1).reshape(width, depth)
    clips = query_lengths.shape[0]
    channels = conv_one.shape[0]
    edge_lanes = -(-time_size * EDGE // LANES) * LANES
    weights, rows, inner_columns, outer_columns, lengths = call(
        functools.partial(tables_kernel, frames, time_size, total_rows),
        "tables",
        (
            wide(19 * channels + SUBLANES, LANES),
            wide(3 * total_rows, LANES),
            wide(SUBLANES, LANES),
            wide(SUBLANES, edge_lanes),
            wide(clips, LANES),
        ),
        index_lengths,
        query_lengths.reshape(1, clips),
        conv_one,
        bias_one.reshape(1, channels),
        conv_two,
        bias_two.reshape(1, 1),
    )
    if cycle_size == 4:
        side = jnp.where(odd, half, 0)
        first = lax.dynamic_slice(flat, (0, half - side), (width, half))
        second = lax.dynamic_slice(flat, (0, side), (width, half))

        def near(t, b):
            return (t, b ^ 2) if t % 2 == 0 else (t, b ^ 1)

        def far(t, b):
            return (t ^ 1, b ^ 2) if t % 2 == 0 else (t ^ 1, b ^ 1)

        near_first = sent(first, near)
        near_second = sent(second, near)
        own = call(own_kernel, "own_maxima", wide(frames, width), index, first, second)
        near_first, own = lax.optimization_barrier((near_first, own))
        far_first = sent(near_first, far)
        next_first = sent(near_first, beside)
        near_second, weights = lax.optimization_barrier((near_second, weights))
        next_second = sent(near_second, beside)
        similar = call(
            functools.partial(near_kernel, block_rows, total_rows),
            "near_similarity",
            wide(total_rows, LANES),
            index, near_first, near_second, own,
        )
        far_first, similar = lax.optimization_barrier((far_first, similar))
        far_second = sent(far_first, beside)
        products = call(
            half_kernel,
            "half_products",
            wide(regions * frames, 2 * width),
            index, next_first, far_first,
        )
        count, pieces = 0, (next_second, far_second, products, similar)
    else:
        every = lax.all_gather(flat, "blk")
        count, pieces = cycle_size, [every[b] for b in range(cycle_size)]
    packed = time_size == 8 and total_rows == 4 * SUBLANES and videos <= EDGE
    shape = (SUBLANES, LANES) if packed else (total_rows, message_lanes(time_size, videos)[1])
    message = call(
        functools.partial(late_kernel, count, block_rows, total_rows, videos, packed),
        "late_similarity",
        wide(*shape),
        inner_columns, rows, weights, index, *pieces,
    )

    def swapped(step):
        return sent(message, lambda t, b: (t ^ step, b))

    if packed:
        message = jnp.maximum(message, swapped(1))
        message = jnp.concatenate([message, swapped(2)])
        messages = [message, swapped(4)]
    else:
        step = 1
        while step < time_size:
            messages = [message, swapped(step)]
            message = jnp.maximum(*messages)
            step *= 2
    return call(
        functools.partial(score_kernel, time_size, videos, packed),
        "clip_scores",
        wide(1, clips, videos),
        outer_columns, rows, weights, lengths, *messages,
    )


def solution(mesh):
    placed = (
        P("blk", None, None),
        P("blk", None, "tm", None),
        P(),
        P(),
        P(),
        P(),
        P("blk", None),
        P(),
    )
    return jax.shard_map(
        shards, mesh=mesh, in_specs=placed, out_specs=P("blk", None, None), check_vma=False
    )
```
